32 devices in a mesh: gx: 4 (over x, core), gy: 8 (over z, y).
Axes of the slice: x: 2, y: 2, z: 4, core: 2. Of those that a mesh axis runs over, the one named last changes fastest.
Arguments:
- blade_state: float32 [5, 4, 262144], P(None, 'gx', 'gy'), may hold values from -6 to 6
- back_state: float32 [5, 64, 4096], P(None, 'gx', 'gy'), may hold values from -6 to 6
- blade_cotangent: float32 [5, 4, 262144], P(None, 'gx', 'gy'), may hold values from -6 to 6
- back_cotangent: float32 [5, 64, 4096], P(None, 'gx', 'gy'), may hold values from -6 to 6
- blade_flux: float32 [3, 5, 5], replicated, may hold values from -3 to 3
- back_flux: float32 [3, 5, 5], replicated, may hold values from -3 to 3
- blade_owner: int32 [2, 32768, 1], P(None, ('gx', 'gy')), may hold values from 0 to 31; in each aligned block of 1024 rows (0 to 1023, 1024 to 2047, ..., all dimensions but the last counted through in order) at most 64 rows name the same one
- back_donor_cell: int32 [2, 65536], P(None, ('gx', 'gy')), may hold values from 32 to 7614, as said below
- back_donor_weight: float32 [2, 8, 65536], P(None, None, ('gx', 'gy')), may hold values from 0 to 1, as said below
- hole_cell: int32 [2, 65536], P(None, ('gx', 'gy')), may hold values from 0 to 8159, as said below
- hole_owner: int32 [2, 65536, 1], P(None, ('gx', 'gy')), may hold values from 0 to 31; in each aligned block of 2048 rows (0 to 2047, 2048 to 4095, ..., all dimensions but the last counted through in order) at most 128 rows name the same one
- blade_donor_cell: int32 [2, 131072], P(None, ('gx', 'gy')), may hold values from 0 to 24190, as said below
- blade_donor_weight: float32 [2, 8, 131072], P(None, None, ('gx', 'gy')), may hold values from 0 to 1, as said below
Outputs:
- blade_adjoint: float32 [5, 4, 262144], P(None, 'gx', 'gy')
- back_adjoint: float32 [5, 64, 4096], P(None, 'gx', 'gy')
The draws below stay inside these ranges and needn't reach their ends.
Inputs may be any that keep to these rules, and one draw needn't show every extreme that they name: `blade_owner`: in each step, at most 64 rim receivers of one device name the same owner. `hole_owner`: in each step, at most 128 hole receivers of one device name the same owner. `back_donor_cell`: local cell number (x * 8 + y) * 64 + z of the owner's block with x < 15, y < 7 and 32 <= z < 63. `blade_donor_cell`: local cell number (j * 64 + k) * 128 + i of the owner's blade block with j < 3, k < 61 and i < 127. `hole_cell`: in each step the 2048 cells of one device are distinct local cell numbers (x * 8 + y) * 64 + z of that device with z < 32. `back_donor_weight`: trilinear weights: products of three fractions, nonnegative, summing to one over the 8 corners of each slot. `blade_donor_weight`: trilinear weights: products of three fractions, nonnegative, summing to one over the 8 corners of each slot.
All inputs are finite; a program needn't handle non-finite values.
Results may differ from the reference program's by a relative error of at most 0.0003.
Values sent between devices are 32-bit elements; how exact they have to be, the bound alone decides.
A program may use at most 384 MiB of HBM per device.

```python
import math
import jax
import jax.numpy as jnp
import numpy as np
from jax import lax

WRAP_DEV = 4
WALL_CELLS = 64
CHORD_CELLS = 128
EAST_DEV = 16
NORTH_DEV = 8
VERT_CELLS = 64
HOLE_DEV = 2048
REVERSE_STEPS = 2
BLADES = 4
WRAP_CELLS = 32
EAST_CELLS = 64
NORTH_CELLS = 64
RIM_DEV = 1024
CAP_RIM = 64
CAP_HOLE = 128
RIM_ALL = 32768
HOLE_ALL = 65536
RIM_SLOTS = 65536
HOLE_SLOTS = 131072
N_GX = 4
N_GY = 8


def trilinear(key, slot_count):
    fractions = jax.random.uniform(key, (REVERSE_STEPS, 3, slot_count), jnp.float32)
    corners = []
    for corner in range(8):
        factor = jnp.ones((REVERSE_STEPS, slot_count), jnp.float32)
        for position in range(3):
            picked = corner >> 2 - position & 1
            if picked == 1:
                factor = factor * fractions[:, position]
            else:
                factor = factor * (1.0 - fractions[:, position])
        corners.append(factor)
    return jnp.stack(corners, axis=1)


def draw_back_donor_weight(key, part):
    return trilinear(jax.random.fold_in(key, 11), RIM_SLOTS)


def draw_blade_donor_weight(key, part):
    return trilinear(jax.random.fold_in(key, 12), HOLE_SLOTS)


def draw_back_donor_cell(key, part):
    sub_keys = jax.random.split(jax.random.fold_in(key, 21), 3)
    shape_out = (REVERSE_STEPS, RIM_SLOTS)
    east_pos = jax.random.randint(sub_keys[0], shape_out, 0, EAST_DEV - 1)
    north_pos = jax.random.randint(sub_keys[1], shape_out, 0, NORTH_DEV - 1)
    vert_pos = jax.random.randint(sub_keys[2], shape_out, VERT_CELLS // 2, VERT_CELLS - 1)
    return ((east_pos * NORTH_DEV + north_pos) * VERT_CELLS + vert_pos).astype(jnp.int32)


def draw_blade_donor_cell(key, part):
    sub_keys = jax.random.split(jax.random.fold_in(key, 22), 3)
    shape_out = (REVERSE_STEPS, HOLE_SLOTS)
    wrap_pos = jax.random.randint(sub_keys[0], shape_out, 0, WRAP_DEV - 1)
    wall_pos = jax.random.randint(sub_keys[1], shape_out, 0, WALL_CELLS - 3)
    chord_pos = jax.random.randint(sub_keys[2], shape_out, 0, CHORD_CELLS - 1)
    return ((wrap_pos * WALL_CELLS + wall_pos) * CHORD_CELLS + chord_pos).astype(jnp.int32)


def draw_hole_cell(key, part):
    device_count = HOLE_ALL // HOLE_DEV
    half_vert = VERT_CELLS // 2
    region = EAST_DEV * NORTH_DEV * half_vert
    sub_keys = jax.random.split(jax.random.fold_in(key, 31), REVERSE_STEPS * device_count)
    chosen = jax.vmap(lambda sub_key: jax.random.permutation(sub_key, region)[:HOLE_DEV])(sub_keys)
    chosen = chosen.astype(jnp.int32)
    east_pos = chosen // (NORTH_DEV * half_vert)
    remainder = chosen % (NORTH_DEV * half_vert)
    north_pos = remainder // half_vert
    vert_pos = remainder % half_vert
    cell_list = (east_pos * NORTH_DEV + north_pos) * VERT_CELLS + vert_pos
    return cell_list.reshape(REVERSE_STEPS, HOLE_ALL).astype(jnp.int32)


def shard_levels(stream_key, shape, cuts, least, high):
    level = 1.0
    for dim, blocks in cuts:
        draws = jax.random.uniform(jax.random.fold_in(jax.random.fold_in(stream_key, 6), dim), (blocks,), jnp.float32, least / len(cuts), high / len(cuts))
        level = level * jnp.repeat(jnp.exp(draws), shape[dim] // blocks).reshape((-1,) + (1,) * (len(shape) - 1 - dim))
    return level


def assign_block(key, own, number, rows, count, top, limit, lean):
    sequence = jax.random.permutation(key, count)
    packed, common = load_shares(count, rows * top, limit, lean, True), load_shares(count, rows * top, limit, lean, False)
    places = jnp.arange(count)

    def named(lengths, rotation):
        used = int((lengths > 0).sum())
        fixed = max(1, used // 4)
        passed = fixed + (places - fixed + rotation * (used - fixed)) % max(1, count - fixed)
        return jnp.zeros((count,), jnp.int32).at[sequence[jnp.where(places < fixed, places, passed)]].set(jnp.asarray(lengths, jnp.int32))

    lengths = jnp.where(number % 4 == 0, named(packed, number // 4), named(common, number - number // 4 - 1))
    mixed = jax.random.permutation(jax.random.fold_in(own, 3), count)
    source_of, sink = mixed[0:count // 2 * 2:2], mixed[1:count // 2 * 2:2]
    slack = jnp.minimum(lengths[source_of] - 1, limit - lengths[sink]) // 2
    slack = jnp.where((source_of == sequence[0]) | (sink == sequence[0]) | (lengths[sink] == 0), 0, jnp.maximum(slack, 0))
    passed = jax.random.randint(jax.random.fold_in(own, 4), (count // 2,), 0, 1 << 20) % (slack + 1)
    lengths = lengths.at[source_of].add(-passed).at[sink].add(passed)
    items = jnp.searchsorted(jnp.cumsum(lengths), jnp.arange(rows * top), side="right").astype(jnp.int32)
    table = items.reshape(top, rows).T
    table = table[jax.random.permutation(jax.random.fold_in(own, 1), rows)]
    rotation = jax.random.randint(jax.random.fold_in(own, 2), (rows, 1), 0, top)
    return jnp.take_along_axis(table, (jnp.arange(top)[None, :] + rotation) % top, axis=1)


def load_shares(amount, total, limit, lean, full):
    weights = [(1 << 20) // math.isqrt(standing ** lean) + 1 for standing in range(1, amount + 1)]
    largest = limit if full else min(limit, max(-(-total // amount), total * weights[0] // sum(weights)))
    least = 1 if total - largest >= amount - 1 else 0
    counts, surplus = [largest] + [least] * (amount - 1), total - largest - least * (amount - 1)
    while surplus > 0:
        candidates = [i for i in range(1, amount) if counts[i] < largest] or [i for i in range(1, amount) if counts[i] < limit]
        mass, left = sum([weights[i] for i in candidates]), surplus
        for i in candidates:
            extra = min(limit - counts[i], max(1, left * weights[i] // mass), surplus)
            counts[i] = counts[i] + extra
            surplus = surplus - extra
    return np.array(counts)


def noise(key, dims, width, most, cuts=(), kind=jnp.bfloat16):
    values = jax.random.normal(key, dims, jnp.float32) * width
    if len(cuts) > 0:
        values = shard_levels(key, dims, cuts, -0.22, 0.18) * values
    return jnp.clip(values, min=-most, max=most).astype(kind)


def setup_inputs(seed: int = 0) -> dict:
    arg_keys = jax.random.split(jax.random.key(seed), 14)
    blade_state = noise(arg_keys[0], (5, BLADES, WRAP_CELLS * WALL_CELLS * CHORD_CELLS), 1.0, 6.0, ((1, 4), (2, 8)), jnp.float32)
    back_state = noise(arg_keys[1], (5, EAST_CELLS, NORTH_CELLS * VERT_CELLS), 1.0, 6.0, ((1, 4), (2, 8)), jnp.float32)
    blade_cotangent = noise(arg_keys[2], (5, BLADES, WRAP_CELLS * WALL_CELLS * CHORD_CELLS), 1.0, 6.0, ((1, 4), (2, 8)), jnp.float32)
    back_cotangent = noise(arg_keys[3], (5, EAST_CELLS, NORTH_CELLS * VERT_CELLS), 1.0, 6.0, ((1, 4), (2, 8)), jnp.float32)
    blade_flux = noise(arg_keys[4], (3, 5, 5), 0.5, 3.0, (), jnp.float32)
    back_flux = noise(arg_keys[5], (3, 5, 5), 0.5, 3.0, (), jnp.float32)
    blade_owner_keys = jax.random.split(jax.random.fold_in(arg_keys[6], 1), REVERSE_STEPS * RIM_ALL // RIM_DEV)
    blade_owner_turns = jax.random.permutation(jax.random.fold_in(arg_keys[6], 3), REVERSE_STEPS * RIM_ALL // RIM_DEV)
    blade_owner = jax.vmap(lambda own, number: assign_block(jax.random.fold_in(arg_keys[6], 2), own, number, RIM_DEV, N_GX * N_GY, 1, CAP_RIM, 2))(blade_owner_keys, blade_owner_turns).reshape((REVERSE_STEPS, RIM_ALL, 1))
    back_donor_cell = draw_back_donor_cell(jax.random.fold_in(arg_keys[13], 71), 0)
    back_donor_weight = draw_back_donor_weight(jax.random.fold_in(arg_keys[13], 71), 0)
    hole_cell = draw_hole_cell(jax.random.fold_in(arg_keys[13], 71), 0)
    hole_owner_keys = jax.random.split(jax.random.fold_in(arg_keys[10], 1), REVERSE_STEPS * HOLE_ALL // HOLE_DEV)
    hole_owner_turns = jax.random.permutation(jax.random.fold_in(arg_keys[10], 3), REVERSE_STEPS * HOLE_ALL // HOLE_DEV)
    hole_owner = jax.vmap(lambda own, number: assign_block(jax.random.fold_in(arg_keys[10], 2), own, number, HOLE_DEV, N_GX * N_GY, 1, CAP_HOLE, 2))(hole_owner_keys, hole_owner_turns).reshape((REVERSE_STEPS, HOLE_ALL, 1))
    blade_donor_cell = draw_blade_donor_cell(jax.random.fold_in(arg_keys[13], 71), 0)
    blade_donor_weight = draw_blade_donor_weight(jax.random.fold_in(arg_keys[13], 71), 0)
    return {"blade_state": blade_state, "back_state": back_state, "blade_cotangent": blade_cotangent, "back_cotangent": back_cotangent, "blade_flux": blade_flux, "back_flux": back_flux, "blade_owner": blade_owner, "back_donor_cell": back_donor_cell, "back_donor_weight": back_donor_weight, "hole_cell": hole_cell, "hole_owner": hole_owner, "blade_donor_cell": blade_donor_cell, "blade_donor_weight": blade_donor_weight}


exact_mode = lax.Precision.HIGHEST
time_step = 0.2
damping = 0.1


def face_slice(padded, axis_pos, shift):
    pieces = [slice(None)] * (padded.ndim - 3)
    for position in range(3):
        if position == axis_pos:
            length = padded.shape[padded.ndim - 3 + position] - 2
            pieces.append(slice(shift, shift + length))
        else:
            pieces.append(slice(1, -1))
    return padded[tuple(pieces)]


def flux_apply(matrices, direction, states):
    linear = jnp.einsum("ce,e...->c...", matrices[direction], states, precision=exact_mode)
    return linear + states[1 + direction] * states


def residual_of(padded, matrices):
    center = face_slice(padded, 0, 1)
    summed = jnp.zeros_like(center)
    for direction in range(3):
        upper_side = face_slice(padded, direction, 2)
        lower_side = face_slice(padded, direction, 0)
        summed = summed + 0.5 * (flux_apply(matrices, direction, upper_side) - flux_apply(matrices, direction, lower_side))
        summed = summed - damping * (upper_side - 2.0 * center + lower_side)
    return summed


def adjoint_of(states, padded, matrices):
    center = face_slice(padded, 0, 1)
    summed = jnp.zeros_like(center)
    for direction in range(3):
        upper_side = face_slice(padded, direction, 2)
        lower_side = face_slice(padded, direction, 0)
        jump_half = 0.5 * (lower_side - upper_side)
        turned = jnp.einsum("ec,e...->c...", matrices[direction], jump_half, precision=exact_mode)
        turned = turned + states[1 + direction] * jump_half
        contracted = jnp.sum(states * jump_half, axis=0)
        turned = turned.at[1 + direction].add(contracted)
        summed = summed + turned - damping * (upper_side - 2.0 * center + lower_side)
    return summed


def blade_grid(field_in):
    shaped = field_in.reshape(5, BLADES, WRAP_CELLS, WALL_CELLS, CHORD_CELLS)
    shaped = jnp.pad(shaped, ((0, 0), (0, 0), (1, 1), (0, 0), (0, 0)), mode="wrap")
    return jnp.pad(shaped, ((0, 0), (0, 0), (0, 0), (1, 1), (1, 1)))


def back_grid(field_in):
    shaped = field_in.reshape(5, EAST_CELLS, NORTH_CELLS, VERT_CELLS)
    return jnp.pad(shaped, ((0, 0), (1, 1), (1, 1), (1, 1)))


def blade_split(field_in):
    shaped = field_in.reshape(5, BLADES, N_GY, -1)
    return shaped.transpose(1, 2, 0, 3).reshape(BLADES * N_GY, 5, -1)


def blade_join(blocks):
    shaped = blocks.reshape(BLADES, N_GY, 5, -1)
    return shaped.transpose(2, 0, 1, 3).reshape(5, BLADES, -1)


def back_split(field_in):
    shaped = field_in.reshape(5, N_GX, EAST_DEV, N_GY, NORTH_DEV * VERT_CELLS)
    return shaped.transpose(1, 3, 0, 2, 4).reshape(N_GX * N_GY, 5, -1)


def back_join(blocks):
    shaped = blocks.reshape(N_GX, N_GY, 5, EAST_DEV, NORTH_DEV * VERT_CELLS)
    return shaped.transpose(2, 0, 3, 1, 4).reshape(5, EAST_CELLS, NORTH_CELLS * VERT_CELLS)


def slot_address(owner_rows, capacity):
    def one_device(owner_row):
        ordering = jnp.argsort(owner_row, stable=True).astype(jnp.int32)
        ordered = owner_row[ordering]
        starts = jnp.searchsorted(ordered, ordered, side="left").astype(jnp.int32)
        rank_sorted = jnp.arange(owner_row.shape[0], dtype=jnp.int32) - starts
        rank_list = jnp.zeros_like(owner_row).at[ordering].set(rank_sorted)
        return owner_row * capacity + rank_list
    return jax.vmap(one_device)(owner_rows)


def corner_offset(corner, strides):
    return (corner // 4) * strides[0] + (corner // 2 % 2) * strides[1] + (corner % 2) * strides[2]


def interpolate(blocks, base_cell, weights, strides):
    def one_device(values, base_rows, weight_rows):
        summed = jnp.zeros((values.shape[0], base_rows.shape[0]), jnp.float32)
        for corner in range(8):
            summed = summed + weight_rows[corner][None, :] * values[:, base_rows + corner_offset(corner, strides)]
        return summed
    return jax.vmap(one_device)(blocks, base_cell, weights)


def spread(blocks, base_cell, weights, strides, arrived):
    def one_device(values, base_rows, weight_rows, incoming):
        for corner in range(8):
            values = values.at[:, base_rows + corner_offset(corner, strides)].add(weight_rows[corner][None, :] * incoming)
        return values
    return jax.vmap(one_device)(blocks, base_cell, weights, arrived)


def transfer(sent):
    devices = sent.shape[0]
    return sent.reshape(devices, 5, devices, -1).transpose(2, 1, 0, 3).reshape(devices, 5, -1)


def fill_fringe(blade_blocks, back_blocks, step_table, strides_pair):
    rim_address, hole_address, hole_list, back_base, back_weight, blade_base, blade_weight = step_table
    devices = blade_blocks.shape[0]
    rim_values = transfer(interpolate(back_blocks, back_base, back_weight, strides_pair[1]))
    hole_values = transfer(interpolate(blade_blocks, blade_base, blade_weight, strides_pair[0]))
    rim_fill = jax.vmap(lambda arrived, address: arrived[:, address])(rim_values, rim_address)
    hole_fill = jax.vmap(lambda arrived, address: arrived[:, address])(hole_values, hole_address)
    shaped = blade_blocks.reshape(devices, 5, WRAP_DEV, WALL_CELLS, CHORD_CELLS)
    shaped = shaped.at[:, :, :, WALL_CELLS - 2:, :].set(rim_fill.reshape(devices, 5, WRAP_DEV, 2, CHORD_CELLS))
    back_filled = jax.vmap(lambda values, cell_list, fill_values: values.at[:, cell_list].set(fill_values))(back_blocks, hole_list, hole_fill)
    return shaped.reshape(devices, 5, -1), back_filled


def transpose_fringe(blade_blocks, back_blocks, step_table, strides_pair):
    rim_address, hole_address, hole_list, back_base, back_weight, blade_base, blade_weight = step_table
    devices = blade_blocks.shape[0]
    shaped = blade_blocks.reshape(devices, 5, WRAP_DEV, WALL_CELLS, CHORD_CELLS)
    rim_cot = shaped[:, :, :, WALL_CELLS - 2:, :].reshape(devices, 5, -1)
    blade_kept = shaped.at[:, :, :, WALL_CELLS - 2:, :].set(0.0).reshape(devices, 5, -1)
    rim_sent = jax.vmap(lambda values, address: jnp.zeros((5, 2 * RIM_DEV), jnp.float32).at[:, address].set(values))(rim_cot, rim_address)
    hole_cot = jax.vmap(lambda values, cell_list: values[:, cell_list])(back_blocks, hole_list)
    back_kept = jax.vmap(lambda values, cell_list: values.at[:, cell_list].set(0.0))(back_blocks, hole_list)
    hole_sent = jax.vmap(lambda values, address: jnp.zeros((5, 2 * HOLE_DEV), jnp.float32).at[:, address].set(values))(hole_cot, hole_address)
    rim_arrived = transfer(rim_sent)
    hole_arrived = transfer(hole_sent)
    back_out = spread(back_kept, back_base, back_weight, strides_pair[1], rim_arrived)
    blade_out = spread(blade_kept, blade_base, blade_weight, strides_pair[0], hole_arrived)
    return blade_out, back_out


def reference(blade_state, back_state, blade_cotangent, back_cotangent, blade_flux, back_flux, blade_owner, back_donor_cell, back_donor_weight, hole_cell, hole_owner, blade_donor_cell, blade_donor_weight):
    devices = N_GX * N_GY
    strides_pair = ((WALL_CELLS * CHORD_CELLS, CHORD_CELLS, 1), (NORTH_DEV * VERT_CELLS, VERT_CELLS, 1))
    tables = []
    for step_index in range(REVERSE_STEPS):
        tables.append((
            slot_address(blade_owner[step_index, :, 0].reshape(devices, RIM_DEV), CAP_RIM),
            slot_address(hole_owner[step_index, :, 0].reshape(devices, HOLE_DEV), CAP_HOLE),
            hole_cell[step_index].reshape(devices, HOLE_DEV),
            back_donor_cell[step_index].reshape(devices, 2 * RIM_DEV),
            back_donor_weight[step_index].reshape(8, devices, 2 * RIM_DEV).transpose(1, 0, 2),
            blade_donor_cell[step_index].reshape(devices, 2 * HOLE_DEV),
            blade_donor_weight[step_index].reshape(8, devices, 2 * HOLE_DEV).transpose(1, 0, 2)))
    blade_shape = (5, BLADES, WRAP_CELLS, WALL_CELLS, CHORD_CELLS)
    back_shape = (5, EAST_CELLS, NORTH_CELLS, VERT_CELLS)
    blade_blocks, back_blocks = fill_fringe(blade_split(blade_state), back_split(back_state), tables[0], strides_pair)
    blade_first = blade_join(blade_blocks)
    back_first = back_join(back_blocks)
    blade_next = blade_first - time_step * residual_of(blade_grid(blade_first), blade_flux).reshape(blade_first.shape)
    back_next = back_first - time_step * residual_of(back_grid(back_first), back_flux).reshape(back_first.shape)
    blade_blocks, back_blocks = fill_fringe(blade_split(blade_next), back_split(back_next), tables[1], strides_pair)
    blade_second = blade_join(blade_blocks)
    back_second = back_join(back_blocks)
    blade_mu = blade_cotangent - time_step * adjoint_of(blade_second.reshape(blade_shape), blade_grid(blade_cotangent), blade_flux).reshape(blade_cotangent.shape)
    back_mu = back_cotangent - time_step * adjoint_of(back_second.reshape(back_shape), back_grid(back_cotangent), back_flux).reshape(back_cotangent.shape)
    blade_blocks, back_blocks = transpose_fringe(blade_split(blade_mu), back_split(back_mu), tables[1], strides_pair)
    blade_mid = blade_join(blade_blocks)
    back_mid = back_join(back_blocks)
    blade_mu = blade_mid - time_step * adjoint_of(blade_first.reshape(blade_shape), blade_grid(blade_mid), blade_flux).reshape(blade_mid.shape)
    back_mu = back_mid - time_step * adjoint_of(back_first.reshape(back_shape), back_grid(back_mid), back_flux).reshape(back_mid.shape)
    blade_blocks, back_blocks = transpose_fringe(blade_split(blade_mu), back_split(back_mu), tables[0], strides_pair)
    return blade_join(blade_blocks), back_join(back_blocks)
```

```python
import functools

import jax
import jax.numpy as jnp
from jax import lax
from jax.experimental import pallas as pl
from jax.experimental.pallas import tpu as pltpu
from jax.sharding import PartitionSpec as P

WRAP_DEV = 4
WALL_CELLS = 64
CHORD_CELLS = 128
EAST_DEV = 16
NORTH_DEV = 8
VERT_CELLS = 64
HOLE_DEV = 2048
REVERSE_STEPS = 2
RIM_DEV = 1024


exact_mode = lax.Precision.HIGHEST
time_step = 0.2
damping = 0.1


def padded_2(block, sides, width, periodic):
    for axis, dim in sides:
        count = lax.axis_size(axis)
        forward = [(i, i + 1) for i in range(count - 1)]
        if periodic:
            forward.append((count - 1, 0))
        backward = [(target, source) for source, target in forward]
        low = lax.ppermute(
            lax.slice_in_dim(block, block.shape[dim] - width, None, axis=dim), axis, forward
        )
        high = lax.ppermute(lax.slice_in_dim(block, 0, width, axis=dim), axis, backward)
        block = jnp.concatenate([low, block, high], axis=dim)
    return block


def face_slice(padded, axis_pos, shift):
    pieces = [slice(None)] * (padded.ndim - 3)
    for position in range(3):
        if position == axis_pos:
            length = padded.shape[padded.ndim - 3 + position] - 2
            pieces.append(slice(shift, shift + length))
        else:
            pieces.append(slice(1, -1))
    return padded[tuple(pieces)]


def flux_apply(matrices, direction, states):
    linear = jnp.einsum("ce,e...->c...", matrices[direction], states, precision=exact_mode)
    return linear + states[1 + direction] * states


def residual_of(padded, matrices):
    center = face_slice(padded, 0, 1)
    summed = jnp.zeros_like(center)
    for direction in range(3):
        upper_side = face_slice(padded, direction, 2)
        lower_side = face_slice(padded, direction, 0)
        summed = summed + 0.5 * (
            flux_apply(matrices, direction, upper_side)
            - flux_apply(matrices, direction, lower_side)
        )
        summed = summed - damping * (upper_side - 2.0 * center + lower_side)
    return summed


def adjoint_of(states, padded, matrices):
    center = face_slice(padded, 0, 1)
    summed = jnp.zeros_like(center)
    for direction in range(3):
        upper_side = face_slice(padded, direction, 2)
        lower_side = face_slice(padded, direction, 0)
        jump_half = 0.5 * (lower_side - upper_side)
        turned = jnp.einsum("ec,e...->c...", matrices[direction], jump_half, precision=exact_mode)
        turned = turned + states[1 + direction] * jump_half
        contracted = jnp.sum(states * jump_half, axis=0)
        chosen = jnp.arange(5).reshape(5, 1, 1, 1) == 1 + direction
        turned = turned + jnp.where(chosen, contracted[None], 0.0)
        summed = summed + turned - damping * (upper_side - 2.0 * center + lower_side)
    return summed


def blade_padded(flat_field):
    shaped = flat_field.reshape(5, WRAP_DEV, WALL_CELLS, CHORD_CELLS)
    widened = padded_2(shaped, (("gy", 1),), 1, True)
    return jnp.pad(widened, ((0, 0), (0, 0), (1, 1), (1, 1)))


def back_padded(flat_field):
    shaped = flat_field.reshape(5, EAST_DEV, NORTH_DEV, VERT_CELLS)
    widened = padded_2(shaped, (("gx", 1), ("gy", 2)), 1, False)
    return jnp.pad(widened, ((0, 0), (0, 0), (0, 0), (1, 1)))


def slot_address(owners, capacity, devices):
    count = owners.shape[0]
    owner_marks = (owners[:, None] == jnp.arange(devices, dtype=jnp.int32)[None, :]).astype(
        jnp.bfloat16
    )
    positions = jnp.arange(count, dtype=jnp.int32)
    lower_ones = (positions[:, None] > positions[None, :]).astype(jnp.bfloat16)
    before = jnp.dot(lower_ones, owner_marks, preferred_element_type=jnp.float32)
    rank_list = jnp.sum(before * owner_marks.astype(jnp.float32), axis=1).astype(jnp.int32)
    return owners * capacity + rank_list


def dot_plain(left, right):
    return lax.dot_general(left, right, (((1,), (0,)), ((), ())), preferred_element_type=jnp.float32)


def dot_slots(left, right):
    return lax.dot_general(left, right, (((1,), (1,)), ((), ())), preferred_element_type=jnp.float32)


def halves(values):
    upper = values.astype(jnp.bfloat16)
    return upper, (values - upper.astype(jnp.float32)).astype(jnp.bfloat16)


def marks(base, weights, rows, cols, step):
    count = base.shape[1]
    shift = cols.bit_length() - 1
    row_off = lax.broadcasted_iota(jnp.int32, (rows, count), 0) - lax.shift_right_arithmetic(
        base, shift
    )
    col_off = lax.broadcasted_iota(jnp.int32, (cols, count), 0) - (base & (cols - 1))
    if weights is None:
        row_marks = jnp.where(row_off == 0, 1.0, 0.0)
        col_marks = jnp.where(col_off == 0, 1.0, 0.0)
        return row_marks, col_marks
    w = [weights[k : k + 1, :] for k in range(8)]
    row_marks = jnp.where(row_off == 0, w[0] + w[1], 0.0)
    row_marks = jnp.where(row_off == 1, w[2] + w[3], row_marks)
    row_marks = jnp.where(row_off == step, w[4] + w[5], row_marks)
    row_marks = jnp.where(row_off == step + 1, w[6] + w[7], row_marks)
    col_marks = jnp.where(col_off == 0, (w[0] + w[2]) + (w[4] + w[6]), 0.0)
    col_marks = jnp.where(col_off == 1, (w[1] + w[3]) + (w[5] + w[7]), col_marks)
    return row_marks, col_marks


def pick_kernel(shape, step, weighted, *refs):
    parts, rows, cols = shape
    field_ref, base_ref = refs[:2]
    out_ref = refs[-1]
    row_marks, col_marks = marks(
        base_ref[...], refs[2][...] if weighted else None, rows, cols, step
    )
    row_high, row_low = halves(row_marks)
    field_high, field_low = halves(field_ref[...])
    mixed = dot_plain(field_high, row_high) + dot_plain(field_low, row_high)
    if weighted:
        mixed = mixed + dot_plain(field_high, row_low)
    for part in range(parts):
        piece = mixed[part * cols : (part + 1) * cols, :] * col_marks
        out_ref[part : part + 1, :] = jnp.sum(piece, axis=0, keepdims=True)


def place_kernel(shape, step, weighted, *refs):
    parts, rows, cols = shape
    values_ref, base_ref = refs[:2]
    out_ref = refs[-1]
    row_marks, col_marks = marks(
        base_ref[...], refs[2][...] if weighted else None, rows, cols, step
    )
    row_high, row_low = halves(row_marks)
    terms = jnp.concatenate(
        [col_marks * values_ref[part : part + 1, :] for part in range(parts)], axis=0
    )
    term_high, term_low = halves(terms)
    total = dot_slots(row_high, term_high) + dot_slots(row_high, term_low)
    if weighted:
        total = total + dot_slots(row_low, term_high)

    @pl.when(pl.program_id(0) == 0)
    def _():
        out_ref[...] = jnp.zeros_like(out_ref)

    out_ref[...] += total


def slot_specs(width, weighted):
    specs = [pl.BlockSpec((1, width), lambda n: (0, n))]
    if weighted:
        specs.append(pl.BlockSpec((8, width), lambda n: (0, n)))
    return specs


def pick(field, base, weights, shape, step=0):
    parts, rows, cols = shape
    count = base.shape[0]
    width = min(count, 512)
    weighted = weights is not None
    extra = (weights,) if weighted else ()
    return pl.pallas_call(
        functools.partial(pick_kernel, shape, step, weighted),
        grid=(count // width,),
        in_specs=[pl.BlockSpec((parts * cols, rows), lambda n: (0, 0))]
        + slot_specs(width, weighted),
        out_specs=pl.BlockSpec((parts, width), lambda n: (0, n)),
        out_shape=jax.ShapeDtypeStruct((parts, count), jnp.float32),
        compiler_params=pltpu.CompilerParams(vmem_limit_bytes=40 * 2**20),
    )(field, base[None, :], *extra)


def place(values, base, weights, shape, step=0):
    parts, rows, cols = shape
    count = base.shape[0]
    width = min(count, 1024)
    weighted = weights is not None
    extra = (weights,) if weighted else ()
    return pl.pallas_call(
        functools.partial(place_kernel, shape, step, weighted),
        grid=(count // width,),
        in_specs=[pl.BlockSpec((parts, width), lambda n: (0, n))] + slot_specs(width, weighted),
        out_specs=pl.BlockSpec((rows, parts * cols), lambda n: (0, 0)),
        out_shape=jax.ShapeDtypeStruct((rows, parts * cols), jnp.float32),
        compiler_params=pltpu.CompilerParams(vmem_limit_bytes=40 * 2**20),
    )(values, base[None, :], *extra)


BLADE_ROWS = (5, WRAP_DEV * WALL_CELLS, CHORD_CELLS)
BACK_ROWS = (5, EAST_DEV * NORTH_DEV, VERT_CELLS)


def field_columns(flat_field, shape):
    return flat_field.reshape(shape).transpose(0, 2, 1).reshape(shape[0] * shape[2], shape[1])


def field_flat(placed, shape):
    return placed.reshape(shape[1], shape[0], shape[2]).transpose(1, 0, 2).reshape(shape[0], -1)


def exchange(rows):
    return lax.all_to_all(rows, ("gx", "gy"), split_axis=0, concat_axis=0, tiled=True)


def slot_cells(hole_list, hole_address, devices):
    capacity = 2 * HOLE_DEV // devices
    described = jnp.stack(
        [hole_list // VERT_CELLS, hole_list % VERT_CELLS, jnp.ones_like(hole_list)]
    ).astype(jnp.float32)
    placed = place(described, hole_address, None, (3, devices, capacity))
    found = field_flat(placed, (3, devices, capacity)).astype(jnp.int32)
    return jnp.where(found[2] > 0, found[0] * VERT_CELLS + found[1], -1)


def fill_fringe(blade_flat, back_flat, step_table):
    rim_address, slot_list, back_base, back_weight, blade_base, blade_weight = step_table
    devices = lax.axis_size("gx") * lax.axis_size("gy")
    rim_capacity = 2 * RIM_DEV // devices
    hole_capacity = 2 * HOLE_DEV // devices
    rim_values = pick(
        field_columns(back_flat, BACK_ROWS), back_base, back_weight, BACK_ROWS, NORTH_DEV
    )
    hole_values = pick(
        field_columns(blade_flat, BLADE_ROWS), blade_base, blade_weight, BLADE_ROWS, WALL_CELLS
    )
    sent = jnp.concatenate(
        [rim_values.reshape(5, devices, -1), hole_values.reshape(5, devices, -1)], axis=2
    )
    arrived = exchange(sent.transpose(1, 0, 2).reshape(devices, -1))
    arrived = arrived.reshape(devices, 5, rim_capacity + hole_capacity)
    rim_arrived = arrived[:, :, :rim_capacity].reshape(devices, -1).T
    rim_fill = pick(rim_arrived, rim_address, None, (5, devices, rim_capacity))
    shaped = blade_flat.reshape(5, WRAP_DEV, WALL_CELLS, CHORD_CELLS)
    shaped = jnp.concatenate(
        [shaped[:, :, : WALL_CELLS - 2], rim_fill.reshape(5, WRAP_DEV, 2, CHORD_CELLS)], axis=2
    )
    hole_arrived = arrived[:, :, rim_capacity:].transpose(1, 0, 2).reshape(5, -1)
    hole_arrived = jnp.concatenate(
        [hole_arrived, jnp.ones((1, 2 * HOLE_DEV), jnp.float32)], axis=0
    )
    shape = (6,) + BACK_ROWS[1:]
    placed = field_flat(place(hole_arrived, slot_list, None, shape), shape)
    holes = placed[5] > 0.5
    back_filled = jnp.where(holes[None], placed[:5], back_flat)
    return (shaped.reshape(5, -1), back_filled, holes)


def transpose_fringe(blade_flat, back_flat, step_table, holes):
    rim_address, slot_list, back_base, back_weight, blade_base, blade_weight = step_table
    devices = lax.axis_size("gx") * lax.axis_size("gy")
    rim_capacity = 2 * RIM_DEV // devices
    hole_capacity = 2 * HOLE_DEV // devices
    shaped = blade_flat.reshape(5, WRAP_DEV, WALL_CELLS, CHORD_CELLS)
    rim_cot = shaped[:, :, WALL_CELLS - 2 :, :].reshape(5, -1)
    blade_kept = jnp.where(
        jnp.arange(WALL_CELLS)[:, None] < WALL_CELLS - 2, shaped, 0.0
    ).reshape(5, -1)
    rim_sent = place(rim_cot, rim_address, None, (5, devices, rim_capacity))
    hole_sent = pick(field_columns(back_flat, BACK_ROWS), slot_list, None, BACK_ROWS)
    back_kept = jnp.where(holes[None], 0.0, back_flat)
    sent = jnp.concatenate(
        [
            rim_sent.reshape(devices, 5, rim_capacity),
            hole_sent.reshape(5, devices, hole_capacity).transpose(1, 0, 2),
        ],
        axis=2,
    )
    arrived = exchange(sent.reshape(devices, -1)).reshape(devices, 5, -1).transpose(1, 0, 2)
    rim_arrived = arrived[:, :, :rim_capacity].reshape(5, -1)
    hole_arrived = arrived[:, :, rim_capacity:].reshape(5, -1)
    back_out = back_kept + field_flat(
        place(rim_arrived, back_base, back_weight, BACK_ROWS, NORTH_DEV), BACK_ROWS
    )
    blade_out = blade_kept + field_flat(
        place(hole_arrived, blade_base, blade_weight, BLADE_ROWS, WALL_CELLS), BLADE_ROWS
    )
    return (blade_out, back_out)


def body(
    blade_state,
    back_state,
    blade_cotangent,
    back_cotangent,
    blade_flux,
    back_flux,
    blade_owner,
    back_donor_cell,
    back_donor_weight,
    hole_cell,
    hole_owner,
    blade_donor_cell,
    blade_donor_weight,
):
    devices = lax.axis_size("gx") * lax.axis_size("gy")
    rim_capacity = 2 * RIM_DEV // devices
    hole_capacity = 2 * HOLE_DEV // devices
    tables = []
    for step_index in range(REVERSE_STEPS):
        tables.append(
            (
                slot_address(blade_owner[step_index, :, 0], rim_capacity, devices),
                slot_cells(
                    hole_cell[step_index],
                    slot_address(hole_owner[step_index, :, 0], hole_capacity, devices),
                    devices,
                ),
                back_donor_cell[step_index],
                back_donor_weight[step_index],
                blade_donor_cell[step_index],
                blade_donor_weight[step_index],
            )
        )
    blade_shape = (5, WRAP_DEV, WALL_CELLS, CHORD_CELLS)
    back_shape = (5, EAST_DEV, NORTH_DEV, VERT_CELLS)
    blade_first, back_first, first_holes = fill_fringe(
        blade_state[:, 0], back_state.reshape(5, -1), tables[0]
    )
    blade_next = blade_first - time_step * residual_of(
        blade_padded(blade_first), blade_flux
    ).reshape(5, -1)
    back_next = back_first - time_step * residual_of(back_padded(back_first), back_flux).reshape(
        5, -1
    )
    blade_second, back_second, second_holes = fill_fringe(blade_next, back_next, tables[1])
    blade_cot = blade_cotangent[:, 0]
    back_cot = back_cotangent.reshape(5, -1)
    blade_mu = blade_cot - time_step * adjoint_of(
        blade_second.reshape(blade_shape), blade_padded(blade_cot), blade_flux
    ).reshape(5, -1)
    back_mu = back_cot - time_step * adjoint_of(
        back_second.reshape(back_shape), back_padded(back_cot), back_flux
    ).reshape(5, -1)
    blade_mid, back_mid = transpose_fringe(blade_mu, back_mu, tables[1], second_holes)
    blade_mu = blade_mid - time_step * adjoint_of(
        blade_first.reshape(blade_shape), blade_padded(blade_mid), blade_flux
    ).reshape(5, -1)
    back_mu = back_mid - time_step * adjoint_of(
        back_first.reshape(back_shape), back_padded(back_mid), back_flux
    ).reshape(5, -1)
    blade_last, back_last = transpose_fringe(blade_mu, back_mu, tables[0], first_holes)
    return (blade_last.reshape(blade_state.shape), back_last.reshape(back_state.shape))


def solution(mesh):
    return jax.shard_map(
        body,
        mesh=mesh,
        in_specs=(
            P(None, "gx", "gy"),
            P(None, "gx", "gy"),
            P(None, "gx", "gy"),
            P(None, "gx", "gy"),
            P(),
            P(),
            P(None, ("gx", "gy"), None),
            P(None, ("gx", "gy")),
            P(None, None, ("gx", "gy")),
            P(None, ("gx", "gy")),
            P(None, ("gx", "gy"), None),
            P(None, ("gx", "gy")),
            P(None, None, ("gx", "gy")),
        ),
        out_specs=(P(None, "gx", "gy"), P(None, "gx", "gy")),
        check_vma=False,
    )
```

```python
import functools

import jax
import jax.numpy as jnp
from jax import lax
from jax.experimental import pallas as pl
from jax.experimental.pallas import tpu as pltpu
from jax.sharding import PartitionSpec as P

WRAP_DEV = 4
WALL_CELLS = 64
CHORD_CELLS = 128
EAST_DEV = 16
NORTH_DEV = 8
VERT_CELLS = 64
HOLE_DEV = 2048
REVERSE_STEPS = 2
RIM_DEV = 1024


exact_mode = lax.Precision.HIGHEST
time_step = 0.2
damping = 0.1


def padded_2(block, sides, width, periodic):
    for axis, dim in sides:
        count = lax.axis_size(axis)
        forward = [(i, i + 1) for i in range(count - 1)]
        if periodic:
            forward.append((count - 1, 0))
        backward = [(target, source) for source, target in forward]
        low = lax.ppermute(
            lax.slice_in_dim(block, block.shape[dim] - width, None, axis=dim), axis, forward
        )
        high = lax.ppermute(lax.slice_in_dim(block, 0, width, axis=dim), axis, backward)
        block = jnp.concatenate([low, block, high], axis=dim)
    return block


def face_slice(padded, axis_pos, shift):
    pieces = [slice(None)] * (padded.ndim - 3)
    for position in range(3):
        if position == axis_pos:
            length = padded.shape[padded.ndim - 3 + position] - 2
            pieces.append(slice(shift, shift + length))
        else:
            pieces.append(slice(1, -1))
    return padded[tuple(pieces)]


def flux_apply(matrices, direction, states):
    linear = jnp.einsum("ce,e...->c...", matrices[direction], states, precision=exact_mode)
    return linear + states[1 + direction] * states


def residual_of(padded, matrices):
    center = face_slice(padded, 0, 1)
    summed = jnp.zeros_like(center)
    for direction in range(3):
        upper_side = face_slice(padded, direction, 2)
        lower_side = face_slice(padded, direction, 0)
        summed = summed + 0.5 * (
            flux_apply(matrices, direction, upper_side)
            - flux_apply(matrices, direction, lower_side)
        )
        summed = summed - damping * (upper_side - 2.0 * center + lower_side)
    return summed


def adjoint_of(states, padded, matrices):
    center = face_slice(padded, 0, 1)
    summed = jnp.zeros_like(center)
    for direction in range(3):
        upper_side = face_slice(padded, direction, 2)
        lower_side = face_slice(padded, direction, 0)
        jump_half = 0.5 * (lower_side - upper_side)
        turned = jnp.einsum("ec,e...->c...", matrices[direction], jump_half, precision=exact_mode)
        turned = turned + states[1 + direction] * jump_half
        contracted = jnp.sum(states * jump_half, axis=0)
        chosen = jnp.arange(5).reshape(5, 1, 1, 1) == 1 + direction
        turned = turned + jnp.where(chosen, contracted[None], 0.0)
        summed = summed + turned - damping * (upper_side - 2.0 * center + lower_side)
    return summed


def back_padded(flat_field):
    shaped = flat_field.reshape(5, EAST_DEV, NORTH_DEV, VERT_CELLS)
    widened = padded_2(shaped, (("gx", 1), ("gy", 2)), 1, False)
    return jnp.pad(widened, ((0, 0), (0, 0), (0, 0), (1, 1)))


def slot_address(owners, capacity, devices):
    count = owners.shape[0]
    owner_marks = (owners[:, None] == jnp.arange(devices, dtype=jnp.int32)[None, :]).astype(
        jnp.bfloat16
    )
    positions = jnp.arange(count, dtype=jnp.int32)
    lower_ones = (positions[:, None] > positions[None, :]).astype(jnp.bfloat16)
    before = jnp.dot(lower_ones, owner_marks, preferred_element_type=jnp.float32)
    rank_list = jnp.sum(before * owner_marks.astype(jnp.float32), axis=1).astype(jnp.int32)
    return owners * capacity + rank_list


def dot_plain(left, right):
    return lax.dot_general(left, right, (((1,), (0,)), ((), ())), preferred_element_type=jnp.float32)


def dot_slots(left, right):
    return lax.dot_general(left, right, (((1,), (1,)), ((), ())), preferred_element_type=jnp.float32)


def halves(values):
    upper = values.astype(jnp.bfloat16)
    return upper, (values - upper.astype(jnp.float32)).astype(jnp.bfloat16)


def marks(base, weights, rows, cols, step):
    count = base.shape[1]
    shift = cols.bit_length() - 1
    row_off = lax.broadcasted_iota(jnp.int32, (rows, count), 0) - lax.shift_right_arithmetic(
        base, shift
    )
    col_off = lax.broadcasted_iota(jnp.int32, (cols, count), 0) - (base & (cols - 1))
    if weights is None:
        row_marks = jnp.where(row_off == 0, 1.0, 0.0)
        col_marks = jnp.where(col_off == 0, 1.0, 0.0)
        return row_marks, col_marks
    w = [weights[k : k + 1, :] for k in range(8)]
    row_marks = jnp.where(row_off == 0, w[0] + w[1], 0.0)
    row_marks = jnp.where(row_off == 1, w[2] + w[3], row_marks)
    row_marks = jnp.where(row_off == step, w[4] + w[5], row_marks)
    row_marks = jnp.where(row_off == step + 1, w[6] + w[7], row_marks)
    col_marks = jnp.where(col_off == 0, (w[0] + w[2]) + (w[4] + w[6]), 0.0)
    col_marks = jnp.where(col_off == 1, (w[1] + w[3]) + (w[5] + w[7]), col_marks)
    return row_marks, col_marks


def pick_kernel(shape, step, weighted, *refs):
    parts, rows, cols = shape
    field_ref, base_ref = refs[:2]
    out_ref = refs[-1]
    row_marks, col_marks = marks(
        base_ref[...], refs[2][...] if weighted else None, rows, cols, step
    )
    row_high, row_low = halves(row_marks)
    field_high, field_low = halves(field_ref[...])
    if weighted:
        mixed = dot_plain(
            jnp.concatenate([field_high, field_low, field_high], axis=1),
            jnp.concatenate([row_high, row_high, row_low], axis=0),
        )
    else:
        mixed = dot_plain(field_high, row_high) + dot_plain(field_low, row_high)
    for part in range(parts):
        piece = mixed[part * cols : (part + 1) * cols, :] * col_marks
        out_ref[part : part + 1, :] = jnp.sum(piece, axis=0, keepdims=True)


def place_kernel(shape, step, weighted, *refs):
    parts, rows, cols = shape
    values_ref, base_ref = refs[:2]
    out_ref = refs[-1]
    row_marks, col_marks = marks(
        base_ref[...], refs[2][...] if weighted else None, rows, cols, step
    )
    row_high, row_low = halves(row_marks)
    terms = jnp.concatenate(
        [col_marks * values_ref[part : part + 1, :] for part in range(parts)], axis=0
    )
    term_high, term_low = halves(terms)
    total = dot_slots(row_high, term_high) + dot_slots(row_high, term_low)
    if weighted:
        total = total + dot_slots(row_low, term_high)

    @pl.when(pl.program_id(0) == 0)
    def _():
        out_ref[...] = jnp.zeros_like(out_ref)

    out_ref[...] += total


def slot_specs(width, weighted):
    specs = [pl.BlockSpec((1, width), lambda n: (0, n))]
    if weighted:
        specs.append(pl.BlockSpec((8, width), lambda n: (0, n)))
    return specs


def pick(field, base, weights, shape, step=0):
    parts, rows, cols = shape
    count = base.shape[0]
    width = min(count, 512)
    weighted = weights is not None
    extra = (weights,) if weighted else ()
    return pl.pallas_call(
        functools.partial(pick_kernel, shape, step, weighted),
        grid=(count // width,),
        in_specs=[pl.BlockSpec((parts * cols, rows), lambda n: (0, 0))]
        + slot_specs(width, weighted),
        out_specs=pl.BlockSpec((parts, width), lambda n: (0, n)),
        out_shape=jax.ShapeDtypeStruct((parts, count), jnp.float32),
        compiler_params=pltpu.CompilerParams(vmem_limit_bytes=40 * 2**20),
    )(field, base[None, :], *extra)


def place(values, base, weights, shape, step=0):
    parts, rows, cols = shape
    count = base.shape[0]
    width = min(count, 1024)
    weighted = weights is not None
    extra = (weights,) if weighted else ()
    return pl.pallas_call(
        functools.partial(place_kernel, shape, step, weighted),
        grid=(count // width,),
        in_specs=[pl.BlockSpec((parts, width), lambda n: (0, n))] + slot_specs(width, weighted),
        out_specs=pl.BlockSpec((rows, parts * cols), lambda n: (0, 0)),
        out_shape=jax.ShapeDtypeStruct((rows, parts * cols), jnp.float32),
        compiler_params=pltpu.CompilerParams(vmem_limit_bytes=40 * 2**20),
    )(values, base[None, :], *extra)


BLADE_ROWS = (5, WRAP_DEV * WALL_CELLS, CHORD_CELLS)
BACK_ROWS = (5, EAST_DEV * NORTH_DEV, VERT_CELLS)


def field_columns(flat_field, shape):
    return flat_field.reshape(shape).transpose(0, 2, 1).reshape(shape[0] * shape[2], shape[1])


def field_flat(placed, shape):
    return placed.reshape(shape[1], shape[0], shape[2]).transpose(1, 0, 2).reshape(shape[0], -1)


def exchange(rows):
    return lax.all_to_all(rows, ("gx", "gy"), split_axis=0, concat_axis=0, tiled=True)


def slot_cells(hole_list, hole_address, devices):
    capacity = 2 * HOLE_DEV // devices
    described = jnp.stack(
        [hole_list // VERT_CELLS, hole_list % VERT_CELLS, jnp.ones_like(hole_list)]
    ).astype(jnp.float32)
    placed = place(described, hole_address, None, (3, devices, capacity))
    found = field_flat(placed, (3, devices, capacity)).astype(jnp.int32)
    return jnp.where(found[2] > 0, found[0] * VERT_CELLS + found[1], -1)


def fill_fringe(blade_flat, back_flat, step_table):
    rim_address, slot_list, back_base, back_weight, blade_base, blade_weight = step_table
    devices = lax.axis_size("gx") * lax.axis_size("gy")
    rim_capacity = 2 * RIM_DEV // devices
    hole_capacity = 2 * HOLE_DEV // devices
    rim_values = pick(
        field_columns(back_flat, BACK_ROWS), back_base, back_weight, BACK_ROWS, NORTH_DEV
    )
    hole_values = pick(
        field_columns(blade_flat, BLADE_ROWS), blade_base, blade_weight, BLADE_ROWS, WALL_CELLS
    )
    sent = jnp.concatenate(
        [rim_values.reshape(5, devices, -1), hole_values.reshape(5, devices, -1)], axis=2
    )
    arrived = exchange(sent.transpose(1, 0, 2).reshape(devices, -1))
    arrived = arrived.reshape(devices, 5, rim_capacity + hole_capacity)
    rim_arrived = arrived[:, :, :rim_capacity].reshape(devices, -1).T
    rim_fill = pick(rim_arrived, rim_address, None, (5, devices, rim_capacity))
    shaped = blade_flat.reshape(5, WRAP_DEV, WALL_CELLS, CHORD_CELLS)
    shaped = jnp.concatenate(
        [shaped[:, :, : WALL_CELLS - 2], rim_fill.reshape(5, WRAP_DEV, 2, CHORD_CELLS)], axis=2
    )
    hole_arrived = arrived[:, :, rim_capacity:].transpose(1, 0, 2).reshape(5, -1)
    hole_arrived = jnp.concatenate(
        [hole_arrived, jnp.ones((1, 2 * HOLE_DEV), jnp.float32)], axis=0
    )
    shape = (6,) + BACK_ROWS[1:]
    placed = field_flat(place(hole_arrived, slot_list, None, shape), shape)
    holes = placed[5] > 0.5
    back_filled = jnp.where(holes[None], placed[:5], back_flat)
    return (shaped.reshape(5, -1), back_filled, holes)


def transpose_fringe(blade_flat, back_flat, step_table, holes):
    rim_address, slot_list, back_base, back_weight, blade_base, blade_weight = step_table
    devices = lax.axis_size("gx") * lax.axis_size("gy")
    rim_capacity = 2 * RIM_DEV // devices
    hole_capacity = 2 * HOLE_DEV // devices
    shaped = blade_flat.reshape(5, WRAP_DEV, WALL_CELLS, CHORD_CELLS)
    rim_cot = shaped[:, :, WALL_CELLS - 2 :, :].reshape(5, -1)
    blade_kept = jnp.where(
        jnp.arange(WALL_CELLS)[:, None] < WALL_CELLS - 2, shaped, 0.0
    ).reshape(5, -1)
    rim_sent = place(rim_cot, rim_address, None, (5, devices, rim_capacity))
    hole_sent = pick(field_columns(back_flat, BACK_ROWS), slot_list, None, BACK_ROWS)
    back_kept = jnp.where(holes[None], 0.0, back_flat)
    sent = jnp.concatenate(
        [
            rim_sent.reshape(devices, 5, rim_capacity),
            hole_sent.reshape(5, devices, hole_capacity).transpose(1, 0, 2),
        ],
        axis=2,
    )
    arrived = exchange(sent.reshape(devices, -1)).reshape(devices, 5, -1).transpose(1, 0, 2)
    rim_arrived = arrived[:, :, :rim_capacity].reshape(5, -1)
    hole_arrived = arrived[:, :, rim_capacity:].reshape(5, -1)
    back_out = back_kept + field_flat(
        place(rim_arrived, back_base, back_weight, BACK_ROWS, NORTH_DEV), BACK_ROWS
    )
    blade_out = blade_kept + field_flat(
        place(hole_arrived, blade_base, blade_weight, BLADE_ROWS, WALL_CELLS), BLADE_ROWS
    )
    return (blade_out, back_out)


def blade_kernel(adjoint, *refs):
    flux_ref, field_ref, low_ref, high_ref = refs[:4]
    out_ref = refs[-1]
    planes = field_ref.shape[1]
    size = field_ref.shape[2:]
    places = [lax.broadcasted_iota(jnp.int32, size, axis) for axis in range(2)]
    for plane in range(planes):
        center = [field_ref[c, plane] for c in range(5)]
        states = [refs[4][c, plane] for c in range(5)] if adjoint else None
        totals = [jnp.zeros(size, jnp.float32) for _ in range(5)]
        for t in range(3):
            if t == 0:
                upper = [
                    field_ref[c, plane + 1] if plane + 1 < planes else high_ref[c, 0]
                    for c in range(5)
                ]
                lower = [field_ref[c, plane - 1] if plane > 0 else low_ref[c, 0] for c in range(5)]
            else:
                length = size[t - 1]
                is_last = places[t - 1] == length - 1
                is_first = places[t - 1] == 0
                upper = [
                    jnp.where(is_last, 0.0, pltpu.roll(center[c], length - 1, t - 1))
                    for c in range(5)
                ]
                lower = [
                    jnp.where(is_first, 0.0, pltpu.roll(center[c], 1, t - 1)) for c in range(5)
                ]
            if adjoint:
                jump = [0.5 * (lower[c] - upper[c]) for c in range(5)]
            else:
                jump = [0.5 * (upper[c] - lower[c]) for c in range(5)]
            for c in range(5):
                linear = totals[c] - damping * (upper[c] - 2.0 * center[c] + lower[c])
                for e in range(5):
                    factor = flux_ref[t * 5 + e, c] if adjoint else flux_ref[t * 5 + c, e]
                    linear = linear + factor * jump[e]
                if adjoint:
                    linear = linear + states[1 + t] * jump[c]
                else:
                    linear = linear + 0.5 * (upper[1 + t] * upper[c] - lower[1 + t] * lower[c])
                totals[c] = linear
            if adjoint:
                contracted = states[0] * jump[0]
                for e in range(1, 5):
                    contracted = contracted + states[e] * jump[e]
                totals[1 + t] = totals[1 + t] + contracted
        for c in range(5):
            out_ref[c, plane] = center[c] - time_step * totals[c]


def blade_step(flat_field, matrices, flat_states=None):
    shape = (5, WRAP_DEV, WALL_CELLS, CHORD_CELLS)
    shaped = flat_field.reshape(shape)
    count = lax.axis_size("gy")
    forward = [(i, (i + 1) % count) for i in range(count)]
    backward = [(target, source) for source, target in forward]
    low = lax.ppermute(shaped[:, WRAP_DEV - 1 :], "gy", forward)
    high = lax.ppermute(shaped[:, :1], "gy", backward)
    fields = (shaped, low, high)
    if flat_states is not None:
        fields = fields + (flat_states.reshape(shape),)
    vmem = pl.BlockSpec(memory_space=pltpu.VMEM)
    return pl.pallas_call(
        functools.partial(blade_kernel, flat_states is not None),
        in_specs=[pl.BlockSpec(memory_space=pltpu.SMEM)] + [vmem] * len(fields),
        out_specs=vmem,
        out_shape=jax.ShapeDtypeStruct(shape, jnp.float32),
        compiler_params=pltpu.CompilerParams(vmem_limit_bytes=40 * 2**20),
    )(matrices.reshape(15, 5), *fields).reshape(5, -1)


def body(
    blade_state,
    back_state,
    blade_cotangent,
    back_cotangent,
    blade_flux,
    back_flux,
    blade_owner,
    back_donor_cell,
    back_donor_weight,
    hole_cell,
    hole_owner,
    blade_donor_cell,
    blade_donor_weight,
):
    devices = lax.axis_size("gx") * lax.axis_size("gy")
    rim_capacity = 2 * RIM_DEV // devices
    hole_capacity = 2 * HOLE_DEV // devices
    tables = []
    for step_index in range(REVERSE_STEPS):
        tables.append(
            (
                slot_address(blade_owner[step_index, :, 0], rim_capacity, devices),
                slot_cells(
                    hole_cell[step_index],
                    slot_address(hole_owner[step_index, :, 0], hole_capacity, devices),
                    devices,
                ),
                back_donor_cell[step_index],
                back_donor_weight[step_index],
                blade_donor_cell[step_index],
                blade_donor_weight[step_index],
            )
        )
    back_shape = (5, EAST_DEV, NORTH_DEV, VERT_CELLS)
    blade_first, back_first, first_holes = fill_fringe(
        blade_state[:, 0], back_state.reshape(5, -1), tables[0]
    )
    blade_next = blade_step(blade_first, blade_flux)
    back_next = back_first - time_step * residual_of(back_padded(back_first), back_flux).reshape(
        5, -1
    )
    blade_second, back_second, second_holes = fill_fringe(blade_next, back_next, tables[1])
    blade_cot = blade_cotangent[:, 0]
    back_cot = back_cotangent.reshape(5, -1)
    blade_mu = blade_step(blade_cot, blade_flux, blade_second)
    back_mu = back_cot - time_step * adjoint_of(
        back_second.reshape(back_shape), back_padded(back_cot), back_flux
    ).reshape(5, -1)
    blade_mid, back_mid = transpose_fringe(blade_mu, back_mu, tables[1], second_holes)
    blade_mu = blade_step(blade_mid, blade_flux, blade_first)
    back_mu = back_mid - time_step * adjoint_of(
        back_first.reshape(back_shape), back_padded(back_mid), back_flux
    ).reshape(5, -1)
    blade_last, back_last = transpose_fringe(blade_mu, back_mu, tables[0], first_holes)
    return (blade_last.reshape(blade_state.shape), back_last.reshape(back_state.shape))


def solution(mesh):
    return jax.shard_map(
        body,
        mesh=mesh,
        in_specs=(
            P(None, "gx", "gy"),
            P(None, "gx", "gy"),
            P(None, "gx", "gy"),
            P(None, "gx", "gy"),
            P(),
            P(),
            P(None, ("gx", "gy"), None),
            P(None, ("gx", "gy")),
            P(None, None, ("gx", "gy")),
            P(None, ("gx", "gy")),
            P(None, ("gx", "gy"), None),
            P(None, ("gx", "gy")),
            P(None, None, ("gx", "gy")),
        ),
        out_specs=(P(None, "gx", "gy"), P(None, "gx", "gy")),
        check_vma=False,
    )
```

```python
import functools

import jax
import jax.numpy as jnp
from jax import lax
from jax.experimental import pallas as pl
from jax.experimental.pallas import tpu as pltpu
from jax.sharding import PartitionSpec as P

WRAP_DEV = 4
WALL_CELLS = 64
CHORD_CELLS = 128
EAST_DEV = 16
NORTH_DEV = 8
VERT_CELLS = 64
HOLE_DEV = 2048
REVERSE_STEPS = 2
RIM_DEV = 1024


exact_mode = lax.Precision.HIGHEST
time_step = 0.2
damping = 0.1


def padded_2(block, sides, width, periodic):
    edges = []
    for axis, dim in sides:
        count = lax.axis_size(axis)
        forward = [(i, i + 1) for i in range(count - 1)]
        if periodic:
            forward.append((count - 1, 0))
        backward = [(target, source) for source, target in forward]
        low = lax.ppermute(
            lax.slice_in_dim(block, block.shape[dim] - width, None, axis=dim), axis, forward
        )
        high = lax.ppermute(lax.slice_in_dim(block, 0, width, axis=dim), axis, backward)
        edges.append((dim, low, high))
    for dim, low, high in edges:
        grown = [
            (0, 0) if d == dim else ((block.shape[d] - low.shape[d]) // 2,) * 2
            for d in range(block.ndim)
        ]
        block = jnp.concatenate([jnp.pad(low, grown), block, jnp.pad(high, grown)], axis=dim)
    return block


def face_slice(padded, axis_pos, shift):
    pieces = [slice(None)] * (padded.ndim - 3)
    for position in range(3):
        if position == axis_pos:
            length = padded.shape[padded.ndim - 3 + position] - 2
            pieces.append(slice(shift, shift + length))
        else:
            pieces.append(slice(1, -1))
    return padded[tuple(pieces)]


def flux_apply(matrices, direction, states):
    linear = jnp.einsum("ce,e...->c...", matrices[direction], states, precision=exact_mode)
    return linear + states[1 + direction] * states


def residual_of(padded, matrices):
    center = face_slice(padded, 0, 1)
    summed = jnp.zeros_like(center)
    for direction in range(3):
        upper_side = face_slice(padded, direction, 2)
        lower_side = face_slice(padded, direction, 0)
        summed = summed + 0.5 * (
            flux_apply(matrices, direction, upper_side)
            - flux_apply(matrices, direction, lower_side)
        )
        summed = summed - damping * (upper_side - 2.0 * center + lower_side)
    return summed


def adjoint_of(states, padded, matrices):
    center = face_slice(padded, 0, 1)
    summed = jnp.zeros_like(center)
    for direction in range(3):
        upper_side = face_slice(padded, direction, 2)
        lower_side = face_slice(padded, direction, 0)
        jump_half = 0.5 * (lower_side - upper_side)
        turned = jnp.einsum("ec,e...->c...", matrices[direction], jump_half, precision=exact_mode)
        turned = turned + states[1 + direction] * jump_half
        contracted = jnp.sum(states * jump_half, axis=0)
        chosen = jnp.arange(5).reshape(5, 1, 1, 1) == 1 + direction
        turned = turned + jnp.where(chosen, contracted[None], 0.0)
        summed = summed + turned - damping * (upper_side - 2.0 * center + lower_side)
    return summed


def back_padded(flat_field):
    shaped = flat_field.reshape(5, EAST_DEV, NORTH_DEV, VERT_CELLS)
    widened = padded_2(shaped, (("gx", 1), ("gy", 2)), 1, False)
    return jnp.pad(widened, ((0, 0), (0, 0), (0, 0), (1, 1)))


def slot_address(owners, capacity, devices):
    count = owners.shape[0]
    owner_marks = (owners[:, None] == jnp.arange(devices, dtype=jnp.int32)[None, :]).astype(
        jnp.bfloat16
    )
    positions = jnp.arange(count, dtype=jnp.int32)
    lower_ones = (positions[:, None] > positions[None, :]).astype(jnp.bfloat16)
    before = jnp.dot(lower_ones, owner_marks, preferred_element_type=jnp.float32)
    rank_list = jnp.sum(before * owner_marks.astype(jnp.float32), axis=1).astype(jnp.int32)
    return owners * capacity + rank_list


def dot_plain(left, right):
    return lax.dot_general(left, right, (((1,), (0,)), ((), ())), preferred_element_type=jnp.float32)


def dot_slots(left, right):
    return lax.dot_general(left, right, (((1,), (1,)), ((), ())), preferred_element_type=jnp.float32)


def halves(values):
    upper = values.astype(jnp.bfloat16)
    return upper, (values - upper.astype(jnp.float32)).astype(jnp.bfloat16)


def marks(base, weights, rows, cols, step):
    count = base.shape[1]
    shift = cols.bit_length() - 1
    row_off = lax.broadcasted_iota(jnp.int32, (rows, count), 0) - lax.shift_right_arithmetic(
        base, shift
    )
    col_off = lax.broadcasted_iota(jnp.int32, (cols, count), 0) - (base & (cols - 1))
    if weights is None:
        row_marks = jnp.where(row_off == 0, 1.0, 0.0)
        col_marks = jnp.where(col_off == 0, 1.0, 0.0)
        return row_marks, col_marks
    w = [weights[k : k + 1, :] for k in range(8)]
    row_marks = jnp.where(row_off == 0, w[0] + w[1], 0.0)
    row_marks = jnp.where(row_off == 1, w[2] + w[3], row_marks)
    row_marks = jnp.where(row_off == step, w[4] + w[5], row_marks)
    row_marks = jnp.where(row_off == step + 1, w[6] + w[7], row_marks)
    col_marks = jnp.where(col_off == 0, (w[0] + w[2]) + (w[4] + w[6]), 0.0)
    col_marks = jnp.where(col_off == 1, (w[1] + w[3]) + (w[5] + w[7]), col_marks)
    return row_marks, col_marks


def pick_kernel(shape, step, weighted, *refs):
    parts, rows, cols = shape
    field_ref, base_ref = refs[:2]
    out_ref = refs[-1]
    row_marks, col_marks = marks(
        base_ref[...], refs[2][...] if weighted else None, rows, cols, step
    )
    row_high, row_low = halves(row_marks)
    field_high, field_low = halves(field_ref[...])
    if weighted:
        mixed = dot_plain(
            jnp.concatenate([field_high, field_low, field_high], axis=1),
            jnp.concatenate([row_high, row_high, row_low], axis=0),
        )
    else:
        mixed = dot_plain(field_high, row_high) + dot_plain(field_low, row_high)
    for part in range(parts):
        piece = mixed[part * cols : (part + 1) * cols, :] * col_marks
        out_ref[part : part + 1, :] = jnp.sum(piece, axis=0, keepdims=True)


def place_kernel(shape, step, weighted, *refs):
    parts, rows, cols = shape
    values_ref, base_ref = refs[:2]
    out_ref = refs[-1]
    row_marks, col_marks = marks(
        base_ref[...], refs[2][...] if weighted else None, rows, cols, step
    )
    row_high, row_low = halves(row_marks)
    terms = jnp.concatenate(
        [col_marks * values_ref[part : part + 1, :] for part in range(parts)], axis=0
    )
    term_high, term_low = halves(terms)
    total = dot_slots(row_high, term_high) + dot_slots(row_high, term_low)
    if weighted:
        total = total + dot_slots(row_low, term_high)

    @pl.when(pl.program_id(0) == 0)
    def _():
        out_ref[...] = jnp.zeros_like(out_ref)

    out_ref[...] += total


def slot_specs(width, weighted):
    specs = [pl.BlockSpec((1, width), lambda n: (0, n))]
    if weighted:
        specs.append(pl.BlockSpec((8, width), lambda n: (0, n)))
    return specs


def pick(field, base, weights, shape, step=0):
    parts, rows, cols = shape
    count = base.shape[0]
    width = min(count, 512)
    weighted = weights is not None
    extra = (weights,) if weighted else ()
    return pl.pallas_call(
        functools.partial(pick_kernel, shape, step, weighted),
        grid=(count // width,),
        in_specs=[pl.BlockSpec((parts * cols, rows), lambda n: (0, 0))]
        + slot_specs(width, weighted),
        out_specs=pl.BlockSpec((parts, width), lambda n: (0, n)),
        out_shape=jax.ShapeDtypeStruct((parts, count), jnp.float32),
        compiler_params=pltpu.CompilerParams(vmem_limit_bytes=40 * 2**20),
    )(field, base[None, :], *extra)


def place(values, base, weights, shape, step=0):
    parts, rows, cols = shape
    count = base.shape[0]
    width = min(count, 1024)
    weighted = weights is not None
    extra = (weights,) if weighted else ()
    return pl.pallas_call(
        functools.partial(place_kernel, shape, step, weighted),
        grid=(count // width,),
        in_specs=[pl.BlockSpec((parts, width), lambda n: (0, n))] + slot_specs(width, weighted),
        out_specs=pl.BlockSpec((rows, parts * cols), lambda n: (0, 0)),
        out_shape=jax.ShapeDtypeStruct((rows, parts * cols), jnp.float32),
        compiler_params=pltpu.CompilerParams(vmem_limit_bytes=40 * 2**20),
    )(values, base[None, :], *extra)


BLADE_ROWS = (5, WRAP_DEV * WALL_CELLS, CHORD_CELLS)
BACK_ROWS = (5, EAST_DEV * NORTH_DEV, VERT_CELLS)


def field_columns(flat_field, shape):
    return flat_field.reshape(shape).transpose(0, 2, 1).reshape(shape[0] * shape[2], shape[1])


def field_flat(placed, shape):
    return placed.reshape(shape[1], shape[0], shape[2]).transpose(1, 0, 2).reshape(shape[0], -1)


def exchange(rows):
    return lax.all_to_all(rows, ("gx", "gy"), split_axis=0, concat_axis=0, tiled=True)


def slot_cells(hole_list, hole_address, devices):
    capacity = 2 * HOLE_DEV // devices
    described = jnp.stack(
        [hole_list // VERT_CELLS, hole_list % VERT_CELLS, jnp.ones_like(hole_list)]
    ).astype(jnp.float32)
    placed = place(described, hole_address, None, (3, devices, capacity))
    found = field_flat(placed, (3, devices, capacity)).astype(jnp.int32)
    return jnp.where(found[2] > 0, found[0] * VERT_CELLS + found[1], -1)


def fill_fringe(blade_flat, back_flat, step_table):
    rim_address, slot_list, back_base, back_weight, blade_base, blade_weight = step_table
    devices = lax.axis_size("gx") * lax.axis_size("gy")
    rim_capacity = 2 * RIM_DEV // devices
    hole_capacity = 2 * HOLE_DEV // devices
    rim_values = pick(
        field_columns(back_flat, BACK_ROWS), back_base, back_weight, BACK_ROWS, NORTH_DEV
    )
    hole_values = pick(
        field_columns(blade_flat, BLADE_ROWS), blade_base, blade_weight, BLADE_ROWS, WALL_CELLS
    )
    sent = jnp.concatenate(
        [rim_values.reshape(5, devices, -1), hole_values.reshape(5, devices, -1)], axis=2
    )
    arrived = exchange(sent.transpose(1, 0, 2).reshape(devices, -1))
    arrived = arrived.reshape(devices, 5, rim_capacity + hole_capacity)
    rim_arrived = arrived[:, :, :rim_capacity].reshape(devices, -1).T
    rim_fill = pick(rim_arrived, rim_address, None, (5, devices, rim_capacity))
    shaped = blade_flat.reshape(5, WRAP_DEV, WALL_CELLS, CHORD_CELLS)
    shaped = jnp.concatenate(
        [shaped[:, :, : WALL_CELLS - 2], rim_fill.reshape(5, WRAP_DEV, 2, CHORD_CELLS)], axis=2
    )
    hole_arrived = arrived[:, :, rim_capacity:].transpose(1, 0, 2).reshape(5, -1)
    hole_arrived = jnp.concatenate(
        [hole_arrived, jnp.ones((1, 2 * HOLE_DEV), jnp.float32)], axis=0
    )
    shape = (6,) + BACK_ROWS[1:]
    placed = field_flat(place(hole_arrived, slot_list, None, shape), shape)
    holes = placed[5] > 0.5
    back_filled = jnp.where(holes[None], placed[:5], back_flat)
    return (shaped.reshape(5, -1), back_filled, holes)


def transpose_fringe(blade_flat, back_flat, step_table, holes):
    rim_address, slot_list, back_base, back_weight, blade_base, blade_weight = step_table
    devices = lax.axis_size("gx") * lax.axis_size("gy")
    rim_capacity = 2 * RIM_DEV // devices
    hole_capacity = 2 * HOLE_DEV // devices
    shaped = blade_flat.reshape(5, WRAP_DEV, WALL_CELLS, CHORD_CELLS)
    rim_cot = shaped[:, :, WALL_CELLS - 2 :, :].reshape(5, -1)
    blade_kept = jnp.where(
        jnp.arange(WALL_CELLS)[:, None] < WALL_CELLS - 2, shaped, 0.0
    ).reshape(5, -1)
    rim_sent = place(rim_cot, rim_address, None, (5, devices, rim_capacity))
    hole_sent = pick(field_columns(back_flat, BACK_ROWS), slot_list, None, BACK_ROWS)
    back_kept = jnp.where(holes[None], 0.0, back_flat)
    sent = jnp.concatenate(
        [
            rim_sent.reshape(devices, 5, rim_capacity),
            hole_sent.reshape(5, devices, hole_capacity).transpose(1, 0, 2),
        ],
        axis=2,
    )
    arrived = exchange(sent.reshape(devices, -1)).reshape(devices, 5, -1).transpose(1, 0, 2)
    rim_arrived = arrived[:, :, :rim_capacity].reshape(5, -1)
    hole_arrived = arrived[:, :, rim_capacity:].reshape(5, -1)
    back_out = back_kept + field_flat(
        place(rim_arrived, back_base, back_weight, BACK_ROWS, NORTH_DEV), BACK_ROWS
    )
    blade_out = blade_kept + field_flat(
        place(hole_arrived, blade_base, blade_weight, BLADE_ROWS, WALL_CELLS), BLADE_ROWS
    )
    return (blade_out, back_out)


def blade_kernel(adjoint, *refs):
    flux_ref, field_ref, low_ref, high_ref = refs[:4]
    out_ref = refs[-1]
    planes = field_ref.shape[1]
    size = field_ref.shape[2:]
    places = [lax.broadcasted_iota(jnp.int32, size, axis) for axis in range(2)]
    for plane in range(planes):
        center = [field_ref[c, plane] for c in range(5)]
        states = [refs[4][c, plane] for c in range(5)] if adjoint else None
        totals = [jnp.zeros(size, jnp.float32) for _ in range(5)]
        for t in range(3):
            if t == 0:
                upper = [
                    field_ref[c, plane + 1] if plane + 1 < planes else high_ref[c, 0]
                    for c in range(5)
                ]
                lower = [field_ref[c, plane - 1] if plane > 0 else low_ref[c, 0] for c in range(5)]
            else:
                length = size[t - 1]
                is_last = places[t - 1] == length - 1
                is_first = places[t - 1] == 0
                upper = [
                    jnp.where(is_last, 0.0, pltpu.roll(center[c], length - 1, t - 1))
                    for c in range(5)
                ]
                lower = [
                    jnp.where(is_first, 0.0, pltpu.roll(center[c], 1, t - 1)) for c in range(5)
                ]
            if adjoint:
                jump = [0.5 * (lower[c] - upper[c]) for c in range(5)]
            else:
                jump = [0.5 * (upper[c] - lower[c]) for c in range(5)]
            for c in range(5):
                linear = totals[c] - damping * (upper[c] - 2.0 * center[c] + lower[c])
                for e in range(5):
                    factor = flux_ref[t * 5 + e, c] if adjoint else flux_ref[t * 5 + c, e]
                    linear = linear + factor * jump[e]
                if adjoint:
                    linear = linear + states[1 + t] * jump[c]
                else:
                    linear = linear + 0.5 * (upper[1 + t] * upper[c] - lower[1 + t] * lower[c])
                totals[c] = linear
            if adjoint:
                contracted = states[0] * jump[0]
                for e in range(1, 5):
                    contracted = contracted + states[e] * jump[e]
                totals[1 + t] = totals[1 + t] + contracted
        for c in range(5):
            out_ref[c, plane] = center[c] - time_step * totals[c]


def blade_step(flat_field, matrices, flat_states=None):
    shape = (5, WRAP_DEV, WALL_CELLS, CHORD_CELLS)
    shaped = flat_field.reshape(shape)
    count = lax.axis_size("gy")
    forward = [(i, (i + 1) % count) for i in range(count)]
    backward = [(target, source) for source, target in forward]
    low = lax.ppermute(shaped[:, WRAP_DEV - 1 :], "gy", forward)
    high = lax.ppermute(shaped[:, :1], "gy", backward)
    fields = (shaped, low, high)
    if flat_states is not None:
        fields = fields + (flat_states.reshape(shape),)
    vmem = pl.BlockSpec(memory_space=pltpu.VMEM)
    return pl.pallas_call(
        functools.partial(blade_kernel, flat_states is not None),
        in_specs=[pl.BlockSpec(memory_space=pltpu.SMEM)] + [vmem] * len(fields),
        out_specs=vmem,
        out_shape=jax.ShapeDtypeStruct(shape, jnp.float32),
        compiler_params=pltpu.CompilerParams(vmem_limit_bytes=40 * 2**20),
    )(matrices.reshape(15, 5), *fields).reshape(5, -1)


def body(
    blade_state,
    back_state,
    blade_cotangent,
    back_cotangent,
    blade_flux,
    back_flux,
    blade_owner,
    back_donor_cell,
    back_donor_weight,
    hole_cell,
    hole_owner,
    blade_donor_cell,
    blade_donor_weight,
):
    devices = lax.axis_size("gx") * lax.axis_size("gy")
    rim_capacity = 2 * RIM_DEV // devices
    hole_capacity = 2 * HOLE_DEV // devices
    tables = []
    for step_index in range(REVERSE_STEPS):
        tables.append(
            (
                slot_address(blade_owner[step_index, :, 0], rim_capacity, devices),
                slot_cells(
                    hole_cell[step_index],
                    slot_address(hole_owner[step_index, :, 0], hole_capacity, devices),
                    devices,
                ),
                back_donor_cell[step_index],
                back_donor_weight[step_index],
                blade_donor_cell[step_index],
                blade_donor_weight[step_index],
            )
        )
    back_shape = (5, EAST_DEV, NORTH_DEV, VERT_CELLS)
    blade_first, back_first, first_holes = fill_fringe(
        blade_state[:, 0], back_state.reshape(5, -1), tables[0]
    )
    blade_next = blade_step(blade_first, blade_flux)
    back_next = back_first - time_step * residual_of(back_padded(back_first), back_flux).reshape(
        5, -1
    )
    blade_second, back_second, second_holes = fill_fringe(blade_next, back_next, tables[1])
    blade_cot = blade_cotangent[:, 0]
    back_cot = back_cotangent.reshape(5, -1)
    blade_mu = blade_step(blade_cot, blade_flux, blade_second)
    back_mu = back_cot - time_step * adjoint_of(
        back_second.reshape(back_shape), back_padded(back_cot), back_flux
    ).reshape(5, -1)
    blade_mid, back_mid = transpose_fringe(blade_mu, back_mu, tables[1], second_holes)
    blade_mu = blade_step(blade_mid, blade_flux, blade_first)
    back_mu = back_mid - time_step * adjoint_of(
        back_first.reshape(back_shape), back_padded(back_mid), back_flux
    ).reshape(5, -1)
    blade_last, back_last = transpose_fringe(blade_mu, back_mu, tables[0], first_holes)
    return (blade_last.reshape(blade_state.shape), back_last.reshape(back_state.shape))


def solution(mesh):
    return jax.shard_map(
        body,
        mesh=mesh,
        in_specs=(
            P(None, "gx", "gy"),
            P(None, "gx", "gy"),
            P(None, "gx", "gy"),
            P(None, "gx", "gy"),
            P(),
            P(),
            P(None, ("gx", "gy"), None),
            P(None, ("gx", "gy")),
            P(None, None, ("gx", "gy")),
            P(None, ("gx", "gy")),
            P(None, ("gx", "gy"), None),
            P(None, ("gx", "gy")),
            P(None, None, ("gx", "gy")),
        ),
        out_specs=(P(None, "gx", "gy"), P(None, "gx", "gy")),
        check_vma=False,
    )
```
